32 devices in a mesh: groups: 2 (over y), fsdp: 4 (over z), tp: 2 (over x), sub: 2 (over core).
Axes of the slice: x: 2, y: 2, z: 4, core: 2. Of those that a mesh axis runs over, the one named last changes fastest.
Arguments:
- hidden_acts: bfloat16 [2048, 11008], P(('groups', 'fsdp', 'sub'), 'tp'), parts along dimension 0, may hold values from -6 to 6
- cotangent: bfloat16 [2048, 4096], P(('groups', 'fsdp', 'sub'), 'tp'), parts along dimension 0, may hold values from -6 to 6
- w_down: bfloat16 [11008, 4096], P(('tp', 'fsdp')), may hold values from -0.0546875 to 0.0546875
- projector: bfloat16 [4096, 256], P('tp'), may hold values from -0.09375 to 0.09375
- first_moment: float32 [22016, 256], P(('groups', 'tp', 'fsdp')), parts along dimension 0, may hold values from -0.06 to 0.06
- second_moment: float32 [22016, 256], P(('groups', 'tp', 'fsdp')), parts along dimension 0, may hold values from 1e-06 to 0.0001
Outputs:
- block_out: bfloat16 [2048, 4096], P(('groups', 'fsdp', 'sub'), 'tp'), parts along dimension 0
- acts_grad: bfloat16 [2048, 11008], P(('groups', 'fsdp', 'sub'), 'tp'), parts along dimension 0
- weight_step: float32 [22016, 4096], P(('groups', 'tp', 'fsdp')), parts along dimension 0
- new_first: float32 [22016, 256], P(('groups', 'tp', 'fsdp')), parts along dimension 0
- new_second: float32 [22016, 256], P(('groups', 'tp', 'fsdp')), parts along dimension 0
The draws below stay inside these ranges and needn't reach their ends.
There are 2 independent parts, one for each index of `groups`. The reference program is written for one: setup_inputs(seed, part) draws one part's arguments, and reference() takes and returns one part's arrays. A program takes and returns all parts, laid end to end along the dimension named above; an argument that names none is the same for every part. Nothing has to cross between parts.
All inputs are finite; a program needn't handle non-finite values.
Results may differ from the reference program's by a relative error of at most 0.0052.
Values may be sent and summed in bfloat16 or wider, within the bound.
No kernel may reach another device: no remote copies, remote signals or barrier semaphores. Data moves between devices by JAX's collectives and lax.ppermute only.
A program may use at most 192 MiB of HBM per device.

```python
import math
import jax
import jax.numpy as jnp
from jax import lax

D = 4096
FF = 11008
RANK = 256
TOKENS = 1024
N_TP = 2


def with_spikes(values, key, source, target, shards_of, factor):
    owner, partner = [(jnp.arange(values.shape[position]) // (values.shape[position] // shards_of)).reshape([-1 if axis == position else 1 for axis in range(values.ndim)]) for position in (source, target)]
    chosen = jax.random.permutation(key, shards_of)[partner]
    strong = (owner == chosen) | (owner == (partner + shards_of // 2) % shards_of)
    return jnp.where(strong, factor * values, values)


def block_levels(rng, extent, shards, least, top_value):
    def one(axis_at, parts):
        draws = jax.random.uniform(jax.random.fold_in(jax.random.fold_in(rng, 6), axis_at), (parts,), jnp.float32, least / len(shards), top_value / len(shards))
        return jnp.repeat(jnp.exp(draws), extent[axis_at] // parts).reshape((-1,) + (1,) * (len(extent) - axis_at - 1))

    level = one(*shards[0])
    for cut in shards[1:]:
        level = level * one(*cut)
    return level


def gaussian(own_key, shape, scale, reach, shards=(), dtype=jnp.bfloat16):
    entries = scale * jax.random.normal(own_key, shape, jnp.float32)
    if shards:
        entries = entries * block_levels(own_key, shape, shards, -0.22, 0.18)
    return jnp.clip(entries, -reach, reach).astype(dtype)


def bell_draw_with(stream_key, shape, scale, bound, shards, heavy, kind=jnp.bfloat16):
    values = scale * jax.random.normal(stream_key, shape, jnp.float32)
    if shards:
        values = values * block_levels(stream_key, shape, shards, -0.22, 0.18)
    return jnp.clip(with_spikes(values, jax.random.fold_in(stream_key, 3), *heavy), -bound, bound).astype(kind)


def setup_inputs(seed: int = 0, part: int = 0) -> dict:
    key_list = jax.random.split(jax.random.key(seed), 7)
    part_keys = jax.random.split(jax.random.fold_in(key_list[6], part), 7)
    hidden_acts = bell_draw_with(part_keys[0], (TOKENS, FF), 1.0, 6.0, ((0, 8), (1, 2)), (0, 1, 8, 2.0))
    cotangent = gaussian(part_keys[1], (TOKENS, D), 1.0, 6.0, ((0, 8), (1, 2)))
    w_down = gaussian(key_list[2], (FF, D), FF ** -0.5, 0.0546875, ((0, 8),))
    projector = gaussian(key_list[3], (D, RANK), D ** -0.5, 0.09375, ((0, 2),))
    first_moment = gaussian(part_keys[4], (FF, RANK), 0.01, 0.06, ((0, 8),), jnp.float32)
    second_moment = jnp.clip(jnp.exp(math.log(0.0001) - 4.6051702 * jax.random.uniform(part_keys[5], (FF, RANK), jnp.float32) ** block_levels(part_keys[5], (FF, RANK), ((0, 8),), -0.2, 0.2)), 9.999999974752427e-07, 0.0001)
    return {"hidden_acts": hidden_acts, "cotangent": cotangent, "w_down": w_down, "projector": projector, "first_moment": first_moment, "second_moment": second_moment}


first_decay = 0.9
second_decay = 0.999
first_fix = 1.0 - 0.9 ** 10
second_fix = 1.0 - 0.999 ** 10
epsilon = 1e-08

def reference(hidden_acts, cotangent, w_down, projector, first_moment, second_moment):
    width_tp = FF // N_TP
    summed = jnp.zeros((hidden_acts.shape[0], D), jnp.float32)
    for index in range(N_TP):
        act_block = hidden_acts[:, index * width_tp:(index + 1) * width_tp]
        weight_block = w_down[index * width_tp:(index + 1) * width_tp, :]
        partial_value = jnp.dot(act_block, weight_block, preferred_element_type=jnp.float32).astype(jnp.bfloat16)
        partial_value = lax.optimization_barrier(partial_value)
        summed = summed + partial_value.astype(jnp.float32)
    block_out = summed.astype(jnp.bfloat16)
    acts_grad = jnp.dot(cotangent, w_down.T, preferred_element_type=jnp.float32).astype(jnp.bfloat16)
    coords = jnp.dot(cotangent, projector, preferred_element_type=jnp.float32).astype(jnp.bfloat16)
    projected = jnp.dot(hidden_acts.T, coords, preferred_element_type=jnp.float32) / jnp.float32(hidden_acts.shape[0])
    new_first = first_decay * first_moment + (1.0 - first_decay) * projected
    new_second = second_decay * second_moment + (1.0 - second_decay) * projected * projected
    direction = (new_first / first_fix / (jnp.sqrt(new_second / second_fix) + epsilon)).astype(jnp.bfloat16)
    weight_step = jnp.dot(direction, projector.T, preferred_element_type=jnp.float32)
    return (block_out, acts_grad, weight_step, new_first, new_second)
```

```python
import jax
import jax.numpy as jnp
from jax import lax
from jax.sharding import PartitionSpec as P

first_decay = 0.9
second_decay = 0.999
first_fix = 1.0 - 0.9**10
second_fix = 1.0 - 0.999**10
epsilon = 1e-08

f32 = jnp.float32
bf16 = jnp.bfloat16


def swap(x, axis, bit):
    n = lax.axis_size(axis)
    return lax.ppermute(x, axis, [(i, i ^ bit) for i in range(n)])


def mm(a, b):
    return jnp.dot(a, b, preferred_element_type=f32)


def mm_t(a, b):
    return lax.dot_general(a, b, (((1,), (1,)), ((), ())), preferred_element_type=f32)


def mm_tn(a, b):
    return lax.dot_general(a, b, (((0,), (0,)), ((), ())), preferred_element_type=f32)


def adam_rows(gradient, first_rows, second_rows):
    new_first = first_decay * first_rows + (1.0 - first_decay) * gradient
    new_second = second_decay * second_rows + (1.0 - second_decay) * gradient * gradient
    direction = (new_first / first_fix / (jnp.sqrt(new_second / second_fix) + epsilon)).astype(bf16)
    return direction, new_first, new_second


def halves(x, axis, t):
    n = x.shape[axis] // 2
    return (
        lax.dynamic_slice_in_dim(x, t * n, n, axis),
        lax.dynamic_slice_in_dim(x, (1 - t) * n, n, axis),
    )


def in_order(mine, other, index, axis):
    return jnp.concatenate(
        [jnp.where(index == 0, mine, other), jnp.where(index == 0, other, mine)], axis=axis
    )


def full_basis_of(projector):
    if lax.axis_size("tp") != 2:
        return lax.all_gather(projector, "tp", axis=0, tiled=True)
    t, c = lax.axis_index("tp"), lax.axis_index("sub")
    mine = halves(projector, 0, c)[0]
    got = swap(mine, "tp", 1)
    other = in_order(got, swap(got, "sub", 1), c, 0)
    return in_order(projector, other, t, 0)


def shards(hidden_acts, cotangent, w_down, projector, first_moment, second_moment):
    nz, nx = lax.axis_size("fsdp"), lax.axis_size("tp")
    z, t = lax.axis_index("fsdp"), lax.axis_index("tp")
    rows, width = hidden_acts.shape[0], w_down.shape[0]
    bits = [1 << b for b in range(nz.bit_length() - 1)]
    two = nx == 2

    cot = {0: cotangent}
    for bit in reversed(bits):
        for k in list(cot):
            cot[k ^ bit] = swap(cot[k], "fsdp", bit)
    hid = {}
    for k in range(nz):
        part = lax.dynamic_slice_in_dim(hidden_acts, (z ^ k) * width, width, 1)
        hid[k] = swap(part, "fsdp", k) if k else part

    basis = full_basis_of(projector)
    if two:
        w_mine, w_other = halves(w_down, 1, t)
        b_mine, b_other = halves(basis, 0, t)
        pairs = {k: ((cot[k], w_mine, b_mine), (swap(cot[k], "tp", 1), w_other, b_other)) for k in cot}
    else:
        pairs = {
            k: ((lax.all_gather(cot[k], "tp", axis=1, tiled=True), w_down, basis),) for k in cot
        }

    grads, coords = {}, {}
    for k in cot:
        back = sum(mm_t(c, w) for c, w, _ in pairs[k]).astype(bf16)
        grads[k] = swap(back, "fsdp", k) if k else back
        coords[k] = sum(mm(c, b) for c, _, b in pairs[k]).astype(bf16)
    order = jnp.stack([grads[k] for k in range(nz)])
    acts_grad = jnp.concatenate(
        [lax.dynamic_index_in_dim(order, z ^ j, 0, keepdims=False) for j in range(nz)], axis=1
    )

    outs = {}
    for k in range(nz):
        if two:
            away = mm(hid[k], w_other).astype(bf16)
            outs[k] = mm(hid[k], w_mine) + swap(away, "tp", 1).astype(f32)
        else:
            outs[k] = lax.psum_scatter(
                mm(hid[k], w_down).astype(bf16), "tp", scatter_dimension=1, tiled=True
            ).astype(f32)
    for bit in bits:
        for k in [k for k in outs if k & bit]:
            got = swap(outs.pop(k).astype(bf16), "fsdp", bit)
            outs[k ^ bit] = outs[k ^ bit] + got.astype(f32)
    block_out = outs[0].astype(bf16)

    all_hid = jnp.concatenate([hid[k] for k in range(nz)], axis=0)
    all_coords = jnp.concatenate([coords[k] for k in range(nz)], axis=0)
    local = mm_tn(all_hid, all_coords)
    owned = local + swap(local, "sub", 1)
    token_count = f32(rows * nz * lax.axis_size("sub"))
    direction, new_first, new_second = adam_rows(owned / token_count, first_moment, second_moment)
    weight_step = mm_t(direction, basis)
    return (block_out, acts_grad, weight_step, new_first, new_second)


def solution(mesh):
    in_specs = (
        P(("groups", "fsdp", "sub"), "tp"),
        P(("groups", "fsdp", "sub"), "tp"),
        P(("tp", "fsdp"), None),
        P("tp", None),
        P(("groups", "tp", "fsdp"), None),
        P(("groups", "tp", "fsdp"), None),
    )
    out_specs = (
        P(("groups", "fsdp", "sub"), "tp"),
        P(("groups", "fsdp", "sub"), "tp"),
        P(("groups", "tp", "fsdp"), None),
        P(("groups", "tp", "fsdp"), None),
        P(("groups", "tp", "fsdp"), None),
    )
    return jax.shard_map(shards, mesh=mesh, in_specs=in_specs, out_specs=out_specs, check_vma=False)
```

```python
import jax
import jax.numpy as jnp
from jax import lax
from jax.sharding import PartitionSpec as P

first_decay = 0.9
second_decay = 0.999
first_fix = 1.0 - 0.9**10
second_fix = 1.0 - 0.999**10
epsilon = 1e-08

f32 = jnp.float32
bf16 = jnp.bfloat16


def swap(x, axis, bit):
    n = lax.axis_size(axis)
    return lax.ppermute(x, axis, [(i, i ^ bit) for i in range(n)])


def mm(a, b):
    return jnp.dot(a, b, preferred_element_type=f32)


def mm_t(a, b):
    return lax.dot_general(a, b, (((1,), (1,)), ((), ())), preferred_element_type=f32)


def mm_tn(a, b):
    return lax.dot_general(a, b, (((0,), (0,)), ((), ())), preferred_element_type=f32)


def adam_rows(gradient, first_rows, second_rows):
    new_first = first_decay * first_rows + (1.0 - first_decay) * gradient
    new_second = second_decay * second_rows + (1.0 - second_decay) * gradient * gradient
    direction = (new_first / first_fix / (jnp.sqrt(new_second / second_fix) + epsilon)).astype(bf16)
    return direction, new_first, new_second


def halves(x, axis, t):
    n = x.shape[axis] // 2
    return (
        lax.dynamic_slice_in_dim(x, t * n, n, axis),
        lax.dynamic_slice_in_dim(x, (1 - t) * n, n, axis),
    )


def in_order(mine, other, index, axis):
    return jnp.concatenate(
        [jnp.where(index == 0, mine, other), jnp.where(index == 0, other, mine)], axis=axis
    )


def full_basis_of(projector):
    if lax.axis_size("tp") != 2:
        return lax.all_gather(projector, "tp", axis=0, tiled=True)
    t, c = lax.axis_index("tp"), lax.axis_index("sub")
    mine = halves(projector, 0, c)[0]
    got = swap(mine, "tp", 1)
    other = in_order(got, swap(got, "sub", 1), c, 0)
    return in_order(projector, other, t, 0)


def shards_any(hidden_acts, cotangent, w_down, projector, first_moment, second_moment):
    nz, nx = lax.axis_size("fsdp"), lax.axis_size("tp")
    z, t = lax.axis_index("fsdp"), lax.axis_index("tp")
    rows, width = hidden_acts.shape[0], w_down.shape[0]
    bits = [1 << b for b in range(nz.bit_length() - 1)]
    two = nx == 2

    cot = {0: cotangent}
    for bit in reversed(bits):
        for k in list(cot):
            cot[k ^ bit] = swap(cot[k], "fsdp", bit)
    hid = {}
    for k in range(nz):
        part = lax.dynamic_slice_in_dim(hidden_acts, (z ^ k) * width, width, 1)
        hid[k] = swap(part, "fsdp", k) if k else part

    basis = full_basis_of(projector)
    if two:
        w_mine, w_other = halves(w_down, 1, t)
        b_mine, b_other = halves(basis, 0, t)
        pairs = {k: ((cot[k], w_mine, b_mine), (swap(cot[k], "tp", 1), w_other, b_other)) for k in cot}
    else:
        pairs = {
            k: ((lax.all_gather(cot[k], "tp", axis=1, tiled=True), w_down, basis),) for k in cot
        }

    grads, coords = {}, {}
    for k in cot:
        back = sum(mm_t(c, w) for c, w, _ in pairs[k]).astype(bf16)
        grads[k] = swap(back, "fsdp", k) if k else back
        coords[k] = sum(mm(c, b) for c, _, b in pairs[k]).astype(bf16)
    order = jnp.stack([grads[k] for k in range(nz)])
    acts_grad = jnp.concatenate(
        [lax.dynamic_index_in_dim(order, z ^ j, 0, keepdims=False) for j in range(nz)], axis=1
    )

    outs = {}
    for k in range(nz):
        if two:
            away = mm(hid[k], w_other).astype(bf16)
            outs[k] = mm(hid[k], w_mine) + swap(away, "tp", 1).astype(f32)
        else:
            outs[k] = lax.psum_scatter(
                mm(hid[k], w_down).astype(bf16), "tp", scatter_dimension=1, tiled=True
            ).astype(f32)
    for bit in bits:
        for k in [k for k in outs if k & bit]:
            got = swap(outs.pop(k).astype(bf16), "fsdp", bit)
            outs[k ^ bit] = outs[k ^ bit] + got.astype(f32)
    block_out = outs[0].astype(bf16)

    all_hid = jnp.concatenate([hid[k] for k in range(nz)], axis=0)
    all_coords = jnp.concatenate([coords[k] for k in range(nz)], axis=0)
    local = mm_tn(all_hid, all_coords)
    owned = local + swap(local, "sub", 1)
    token_count = f32(rows * nz * lax.axis_size("sub"))
    direction, new_first, new_second = adam_rows(owned / token_count, first_moment, second_moment)
    weight_step = mm_t(direction, basis)
    return (block_out, acts_grad, weight_step, new_first, new_second)


def after(x, *others):
    return lax.optimization_barrier((x, *others))[0]


def shards_line(hidden_acts, cotangent, w_down, projector, first_moment, second_moment):
    z, t, c = lax.axis_index("fsdp"), lax.axis_index("tp"), lax.axis_index("sub")
    rows, width = hidden_acts.shape[0], w_down.shape[0]

    def own_units(k):
        return lax.dynamic_slice_in_dim(hidden_acts, (z ^ k) * width, width, 1)

    def back(mine, other):
        return (mm_t(mine, w_mine) + mm_t(other, w_other)).astype(bf16)

    def coords(mine, other):
        return (mm(mine, projector) + mm(other, b_other)).astype(bf16)

    w_mine, w_other = halves(w_down, 1, t)
    c0 = cotangent
    c2 = swap(c0, "fsdp", 2)
    half = swap(halves(projector, 0, c)[0], "tp", 1)
    c1 = swap(c0, "fsdp", 1)
    h0, h1, h2, h3 = (own_units(k) for k in range(4))
    h1 = swap(h1, "fsdp", 1)
    away0 = mm(h0, w_other).astype(bf16)

    b_other = in_order(half, swap(half, "sub", 1), c, 0)
    x0 = swap(after(c0, half, away0), "tp", 1)
    h3 = swap(after(h3, c1), "fsdp", 3)
    x2 = swap(c2, "tp", 1)
    c3 = swap(after(c2, h1), "fsdp", 1)
    h2 = swap(after(h2, c2, x0), "fsdp", 2)
    away1 = mm(h1, w_other).astype(bf16)
    x3 = swap(after(c3, x2), "tp", 1)
    a2 = swap(back(c2, x2), "fsdp", 2)
    away3 = mm(h3, w_other).astype(bf16)
    y3 = swap(after(away3, x2), "tp", 1)
    x1 = swap(after(c1, x3), "tp", 1)
    a3 = swap(after(back(c3, x3), h2), "fsdp", 3)
    o3 = mm(h3, w_mine) + y3.astype(f32)
    o3 = swap(o3.astype(bf16), "fsdp", 1)
    away2 = mm(h2, w_other).astype(bf16)
    y2 = swap(after(away2, y3), "tp", 1)
    a1 = swap(after(back(c1, x1), o3), "fsdp", 1)
    y1 = swap(after(away1, x1), "tp", 1)
    o2 = mm(h2, w_mine) + y2.astype(f32) + o3.astype(f32)
    o2 = swap(after(o2.astype(bf16), a2), "fsdp", 2)
    y0 = swap(after(away0, y2), "tp", 1)
    o1 = swap((mm(h1, w_mine) + y1.astype(f32)).astype(bf16), "fsdp", 1)
    a0 = back(c0, x0)

    all_hid = jnp.concatenate([h0, h1, h2, h3], axis=0)
    all_coords = jnp.concatenate([coords(c0, x0), coords(c1, x1), coords(c2, x2), coords(c3, x3)], axis=0)
    local = mm_tn(all_hid, all_coords)
    owned = local + swap(local, "sub", 1)
    token_count = f32(rows * lax.axis_size("fsdp") * lax.axis_size("sub"))
    direction, new_first, new_second = adam_rows(owned / token_count, first_moment, second_moment)
    weight_step = mm_t(direction, in_order(projector, b_other, t, 0))
    o2 = after(o2, weight_step)

    block_out = (mm(h0, w_mine) + y0.astype(f32) + o1.astype(f32) + o2.astype(f32)).astype(bf16)
    order = jnp.stack([a0, a1, a2, a3])
    acts_grad = jnp.concatenate(
        [lax.dynamic_index_in_dim(order, z ^ j, 0, keepdims=False) for j in range(4)], axis=1
    )
    return (block_out, acts_grad, weight_step, new_first, new_second)


def solution(mesh):
    in_specs = (
        P(("groups", "fsdp", "sub"), "tp"),
        P(("groups", "fsdp", "sub"), "tp"),
        P(("tp", "fsdp"), None),
        P("tp", None),
        P(("groups", "tp", "fsdp"), None),
        P(("groups", "tp", "fsdp"), None),
    )
    out_specs = (
        P(("groups", "fsdp", "sub"), "tp"),
        P(("groups", "fsdp", "sub"), "tp"),
        P(("groups", "tp", "fsdp"), None),
        P(("groups", "tp", "fsdp"), None),
        P(("groups", "tp", "fsdp"), None),
    )
    line = mesh.shape["fsdp"] == 4 and mesh.shape["tp"] == 2
    shards = shards_line if line else shards_any
    return jax.shard_map(shards, mesh=mesh, in_specs=in_specs, out_specs=out_specs, check_vma=False)
```

```python
import jax
import jax.numpy as jnp
from jax import lax
from jax.experimental import pallas as pl
from jax.experimental.pallas import tpu as pltpu
from jax.sharding import PartitionSpec as P

first_decay = 0.9
second_decay = 0.999
first_fix = 1.0 - 0.9**10
second_fix = 1.0 - 0.999**10
epsilon = 1e-08

f32 = jnp.float32
bf16 = jnp.bfloat16


def swap(x, axis, bit, name="swap"):
    n = lax.axis_size(axis)
    with jax.named_scope(name):
        return lax.ppermute(x, axis, [(i, i ^ bit) for i in range(n)])


def mm(a, b):
    return jnp.dot(a, b, preferred_element_type=f32)


def mm_t(a, b):
    return lax.dot_general(a, b, (((1,), (1,)), ((), ())), preferred_element_type=f32)


def mm_tn(a, b):
    return lax.dot_general(a, b, (((0,), (0,)), ((), ())), preferred_element_type=f32)


def adam_rows(gradient, first_rows, second_rows):
    new_first = first_decay * first_rows + (1.0 - first_decay) * gradient
    new_second = second_decay * second_rows + (1.0 - second_decay) * gradient * gradient
    direction = (new_first / first_fix / (jnp.sqrt(new_second / second_fix) + epsilon)).astype(bf16)
    return direction, new_first, new_second


def halves(x, axis, t):
    n = x.shape[axis] // 2
    return (
        lax.dynamic_slice_in_dim(x, t * n, n, axis),
        lax.dynamic_slice_in_dim(x, (1 - t) * n, n, axis),
    )


def in_order(mine, other, index, axis):
    return jnp.concatenate(
        [jnp.where(index == 0, mine, other), jnp.where(index == 0, other, mine)], axis=axis
    )


def full_basis_of(projector):
    if lax.axis_size("tp") != 2:
        return lax.all_gather(projector, "tp", axis=0, tiled=True)
    t, c = lax.axis_index("tp"), lax.axis_index("sub")
    mine = halves(projector, 0, c)[0]
    got = swap(mine, "tp", 1)
    other = in_order(got, swap(got, "sub", 1), c, 0)
    return in_order(projector, other, t, 0)


def shards_any(hidden_acts, cotangent, w_down, projector, first_moment, second_moment):
    nz, nx = lax.axis_size("fsdp"), lax.axis_size("tp")
    z, t = lax.axis_index("fsdp"), lax.axis_index("tp")
    rows, width = hidden_acts.shape[0], w_down.shape[0]
    bits = [1 << b for b in range(nz.bit_length() - 1)]
    two = nx == 2

    cot = {0: cotangent}
    for bit in reversed(bits):
        for k in list(cot):
            cot[k ^ bit] = swap(cot[k], "fsdp", bit)
    hid = {}
    for k in range(nz):
        part = lax.dynamic_slice_in_dim(hidden_acts, (z ^ k) * width, width, 1)
        hid[k] = swap(part, "fsdp", k) if k else part

    basis = full_basis_of(projector)
    if two:
        w_mine, w_other = halves(w_down, 1, t)
        b_mine, b_other = halves(basis, 0, t)
        pairs = {k: ((cot[k], w_mine, b_mine), (swap(cot[k], "tp", 1), w_other, b_other)) for k in cot}
    else:
        pairs = {
            k: ((lax.all_gather(cot[k], "tp", axis=1, tiled=True), w_down, basis),) for k in cot
        }

    grads, coords = {}, {}
    for k in cot:
        back = sum(mm_t(c, w) for c, w, _ in pairs[k]).astype(bf16)
        grads[k] = swap(back, "fsdp", k) if k else back
        coords[k] = sum(mm(c, b) for c, _, b in pairs[k]).astype(bf16)
    order = jnp.stack([grads[k] for k in range(nz)])
    acts_grad = jnp.concatenate(
        [lax.dynamic_index_in_dim(order, z ^ j, 0, keepdims=False) for j in range(nz)], axis=1
    )

    outs = {}
    for k in range(nz):
        if two:
            away = mm(hid[k], w_other).astype(bf16)
            outs[k] = mm(hid[k], w_mine) + swap(away, "tp", 1).astype(f32)
        else:
            outs[k] = lax.psum_scatter(
                mm(hid[k], w_down).astype(bf16), "tp", scatter_dimension=1, tiled=True
            ).astype(f32)
    for bit in bits:
        for k in [k for k in outs if k & bit]:
            got = swap(outs.pop(k).astype(bf16), "fsdp", bit)
            outs[k ^ bit] = outs[k ^ bit] + got.astype(f32)
    block_out = outs[0].astype(bf16)

    all_hid = jnp.concatenate([hid[k] for k in range(nz)], axis=0)
    all_coords = jnp.concatenate([coords[k] for k in range(nz)], axis=0)
    local = mm_tn(all_hid, all_coords)
    owned = local + swap(local, "sub", 1)
    token_count = f32(rows * nz * lax.axis_size("sub"))
    direction, new_first, new_second = adam_rows(owned / token_count, first_moment, second_moment)
    weight_step = mm_t(direction, basis)
    return (block_out, acts_grad, weight_step, new_first, new_second)


light = pl.CostEstimate(flops=1, bytes_accessed=1, transcendentals=0)
strip = 512


def in_vmem(kernel, name, at, ins, outs, mib=12):
    vmem = pl.BlockSpec(memory_space=pltpu.VMEM)
    return pl.pallas_call(
        kernel,
        in_specs=[pl.BlockSpec(memory_space=pltpu.SMEM)] + [vmem] * len(ins),
        out_specs=[vmem] * len(outs),
        out_shape=outs,
        compiler_params=pltpu.CompilerParams(vmem_limit_bytes=mib << 20),
        cost_estimate=light,
        name=name,
    )(at, *ins)


def forward(at, h, w):
    rows, width = h.shape[0], w.shape[1]
    half = width // 2

    def kernel(at, h, w, p, m):
        mine, far = at[0] * half, (1 - at[0]) * half
        for j in range(0, half, strip):
            p[:, j : j + strip] = mm(h[...], w[:, pl.ds(pl.multiple_of(far + j, strip), strip)]).astype(bf16)
        for j in range(0, half, strip):
            m[:, j : j + strip] = mm(h[...], w[:, pl.ds(pl.multiple_of(mine + j, strip), strip)])

    return in_vmem(
        kernel, "forward", at, (h, w),
        [jax.ShapeDtypeStruct((rows, half), bf16), jax.ShapeDtypeStruct((rows, half), f32)],
    )


def backward(at, c, x, w, projector, got, shared):
    rows, half = c.shape
    units = w.shape[0]
    part = half // 2
    tall = 352

    def kernel(at, c, x, w, basis, got, shared, g, coords):
        mine = pl.multiple_of(at[0] * half, half)
        far = pl.multiple_of((1 - at[0]) * half, half)
        first = pl.multiple_of(at[1] * part, part)
        second = pl.multiple_of((1 - at[1]) * part, part)
        for j in range(0, units, tall):
            k = min(j + tall, units)
            g[j:k, :] = (
                mm_t(w[j:k, pl.ds(mine, half)], c[...]) + mm_t(w[j:k, pl.ds(far, half)], x[...])
            ).astype(bf16)
        coords[...] = (
            mm(c[...], basis[...])
            + mm(x[:, pl.ds(first, part)], got[...])
            + mm(x[:, pl.ds(second, part)], shared[...])
        ).astype(bf16)

    return in_vmem(
        kernel, "backward", at, (c, x, w, projector, got, shared),
        [
            jax.ShapeDtypeStruct((units, rows), bf16),
            jax.ShapeDtypeStruct((rows, projector.shape[1]), bf16),
        ],
    )


def project(at, hs, coords):
    n, units, rank = len(hs), hs[0].shape[1], coords[0].shape[1]
    tall = units // 2

    def kernel(at, *refs):
        upper, lower = refs[2 * n :]
        total = sum(mm_tn(h[...], c[...]) for h, c in zip(refs[:n], refs[n : 2 * n]))
        upper[...], lower[...] = total[:tall], total[tall:]

    return in_vmem(
        kernel, "project", at, (*hs, *coords), [jax.ShapeDtypeStruct((tall, rank), f32)] * 2
    )


def adam_step(at, here, there, tokens, first_moment, second_moment, projector, got, shared):
    units, rank = first_moment.shape
    half = projector.shape[0]
    part, width = half // 2, 2 * half
    tall = units // 4

    def kernel(at, h_up, h_low, t_up, t_low, first, second, basis, got, shared, step, new_first, new_second):
        upper = pl.program_id(0) < 2
        gradient = jnp.where(upper, h_up[...] + t_up[...], h_low[...] + t_low[...]) / f32(tokens)
        direction, new_first[...], new_second[...] = adam_rows(gradient, first[...], second[...])
        t, c = at[0], at[1]
        mine = pl.multiple_of(t * half, half)
        one = pl.multiple_of((1 - t) * half + c * part, part)
        two = pl.multiple_of((1 - t) * half + (1 - c) * part, part)
        step[:, pl.ds(mine, half)] = mm_t(direction, basis[...])
        step[:, pl.ds(one, part)] = mm_t(direction, got[...])
        step[:, pl.ds(two, part)] = mm_t(direction, shared[...])

    def block(index):
        return pl.BlockSpec((tall, rank), index)

    def up(i):
        return (jnp.minimum(i, 1), 0)

    def low(i):
        return (jnp.maximum(i, 2) - 2, 0)

    def row(i):
        return (i, 0)

    def whole(v):
        return pl.BlockSpec(v.shape, lambda i: (0, 0))

    small = jax.ShapeDtypeStruct((units, rank), f32)
    return pl.pallas_call(
        kernel,
        grid=(4,),
        in_specs=[pl.BlockSpec(memory_space=pltpu.SMEM)]
        + [block(up), block(low), block(up), block(low), block(row), block(row)]
        + [whole(projector), whole(got), whole(shared)],
        out_specs=[pl.BlockSpec((tall, width), row), block(row), block(row)],
        out_shape=[jax.ShapeDtypeStruct((units, width), f32), small, small],
        compiler_params=pltpu.CompilerParams(vmem_limit_bytes=24 << 20),
        cost_estimate=light,
        name="adam_step",
    )(at, *here, *there, first_moment, second_moment, projector, got, shared)


class Order:
    def __init__(self):
        self.last = ()

    def go(self, x):
        return lax.optimization_barrier((x, *self.last))[0]

    def seen(self, *done):
        self.last = done


def shards_line(hidden_acts, cotangent, w_down, projector, first_moment, second_moment):
    z, t, c = lax.axis_index("fsdp"), lax.axis_index("tp"), lax.axis_index("sub")
    rows, width = hidden_acts.shape[0], w_down.shape[0]
    at = jnp.stack([t, c]).astype(jnp.int32)
    tokens = rows * lax.axis_size("fsdp") * lax.axis_size("sub")
    order = Order()
    go, seen = order.go, order.seen

    def own_units(k):
        return lax.dynamic_slice_in_dim(hidden_acts, (z ^ k) * width, width, 1)

    c0 = cotangent
    c2 = swap(c0, "fsdp", 2, "c2")
    x0 = swap(c0, "tp", 1, "x0")
    half = swap(halves(projector, 0, c)[0], "tp", 1, "half")
    c1 = swap(c0, "fsdp", 1, "c1")
    h0, h1, h2, h3 = (own_units(k) for k in range(4))
    h1 = swap(h1, "fsdp", 1, "h1")
    p0, m0 = forward(at, h0, w_down)
    seen(p0, c2, half, c1)
    x2 = swap(go(c2), "tp", 1, "x2")
    h3 = swap(go(h3), "fsdp", 3, "h3")
    c3 = swap(go(c2), "fsdp", 1, "c3")
    basis = swap(go(half), "sub", 1, "basis")
    seen(p0, c1, x0, basis)
    g0, k0 = backward(at, go(c0), x0, w_down, projector, half, basis)
    seen(g0)
    x1 = swap(go(c1), "tp", 1, "x1")
    seen(g0, h1)
    p1, m1 = forward(at, go(h1), w_down)
    seen(p1)
    h2 = swap(go(h2), "fsdp", 2, "h2")
    seen(p1, x2)
    g2, k2 = backward(at, go(c2), x2, w_down, projector, half, basis)
    seen(g2, h3)
    p3, m3 = forward(at, go(h3), w_down)
    seen(p3, c3)
    x3 = swap(go(c3), "tp", 1, "x3")
    seen(p3, c3, x1)
    g1, k1 = backward(at, go(c1), x1, w_down, projector, half, basis)
    a1 = swap(g1, "fsdp", 1, "a1")
    seen(g1, h2)
    y3 = swap(go(p3), "tp", 1, "y3")
    a2 = swap(go(g2), "fsdp", 2, "a2")
    seen(g1, h2)
    p2, m2 = forward(at, go(h2), w_down)
    seen(p2, x3)
    y2 = swap(go(p2), "tp", 1, "y2")
    g3, k3 = backward(at, go(c3), x3, w_down, projector, half, basis)
    a3 = swap(g3, "fsdp", 3, "a3")
    seen(g3, y3, a2, a1)
    o3 = (go(m3) + y3.astype(f32)).astype(bf16)
    r3 = swap(o3, "fsdp", 1, "r3")
    y1 = swap(go(p1), "tp", 1, "y1")
    seen(o3)
    local = project(at, (h0, h1, h2, h3), (go(k0), k1, k2, k3))
    other = [swap(v, "sub", 1, "rows") for v in local]
    seen(local[0], y2, r3, a3)
    o2 = (go(m2) + y2.astype(f32) + r3.astype(f32)).astype(bf16)
    r2 = swap(o2, "fsdp", 2, "r2")
    y0 = swap(go(p0), "tp", 1, "y0")
    by_owner = jnp.stack([go(g0), a1, a2, a3])
    acts_grad = jnp.concatenate(
        [lax.dynamic_index_in_dim(by_owner, z ^ j, 0, keepdims=False) for j in range(4)], axis=0
    ).T
    seen(o2, acts_grad, y1)
    o1 = (go(m1) + y1.astype(f32)).astype(bf16)
    r1 = swap(o1, "fsdp", 1, "r1")
    seen(o1)
    weight_step, new_first, new_second = adam_step(
        at, local, (go(other[0]), other[1]), tokens, first_moment, second_moment, projector, half, basis
    )
    seen(weight_step)
    block_out = (
        go(m0) + y0.astype(f32) + r1.astype(f32) + r2.astype(f32)
    ).astype(bf16)
    return (block_out, acts_grad, weight_step, new_first, new_second)


def solution(mesh):
    in_specs = (
        P(("groups", "fsdp", "sub"), "tp"),
        P(("groups", "fsdp", "sub"), "tp"),
        P(("tp", "fsdp"), None),
        P("tp", None),
        P(("groups", "tp", "fsdp"), None),
        P(("groups", "tp", "fsdp"), None),
    )
    out_specs = (
        P(("groups", "fsdp", "sub"), "tp"),
        P(("groups", "fsdp", "sub"), "tp"),
        P(("groups", "tp", "fsdp"), None),
        P(("groups", "tp", "fsdp"), None),
        P(("groups", "tp", "fsdp"), None),
    )
    line = mesh.shape["fsdp"] == 4 and mesh.shape["tp"] == 2
    shards = shards_line if line else shards_any
    return jax.shard_map(shards, mesh=mesh, in_specs=in_specs, out_specs=out_specs, check_vma=False)
```

```python
import jax
import jax.numpy as jnp
from jax import lax
from jax.experimental import pallas as pl
from jax.experimental.pallas import tpu as pltpu
from jax.sharding import PartitionSpec as P

first_decay = 0.9
second_decay = 0.999
first_fix = 1.0 - 0.9**10
second_fix = 1.0 - 0.999**10
epsilon = 1e-08

f32 = jnp.float32
bf16 = jnp.bfloat16


def swap(x, axis, bit, name="swap"):
    n = lax.axis_size(axis)
    with jax.named_scope(name):
        return lax.ppermute(x, axis, [(i, i ^ bit) for i in range(n)])


def mm(a, b):
    return jnp.dot(a, b, preferred_element_type=f32)


def mm_t(a, b):
    return lax.dot_general(a, b, (((1,), (1,)), ((), ())), preferred_element_type=f32)


def mm_tn(a, b):
    return lax.dot_general(a, b, (((0,), (0,)), ((), ())), preferred_element_type=f32)


def adam_rows(gradient, first_rows, second_rows):
    new_first = first_decay * first_rows + (1.0 - first_decay) * gradient
    new_second = second_decay * second_rows + (1.0 - second_decay) * gradient * gradient
    direction = (new_first / first_fix / (jnp.sqrt(new_second / second_fix) + epsilon)).astype(bf16)
    return direction, new_first, new_second


def halves(x, axis, t):
    n = x.shape[axis] // 2
    return (
        lax.dynamic_slice_in_dim(x, t * n, n, axis),
        lax.dynamic_slice_in_dim(x, (1 - t) * n, n, axis),
    )


def in_order(mine, other, index, axis):
    return jnp.concatenate(
        [jnp.where(index == 0, mine, other), jnp.where(index == 0, other, mine)], axis=axis
    )


def full_basis_of(projector):
    if lax.axis_size("tp") != 2:
        return lax.all_gather(projector, "tp", axis=0, tiled=True)
    t, c = lax.axis_index("tp"), lax.axis_index("sub")
    mine = halves(projector, 0, c)[0]
    got = swap(mine, "tp", 1)
    other = in_order(got, swap(got, "sub", 1), c, 0)
    return in_order(projector, other, t, 0)


def shards_any(hidden_acts, cotangent, w_down, projector, first_moment, second_moment):
    nz, nx = lax.axis_size("fsdp"), lax.axis_size("tp")
    z, t = lax.axis_index("fsdp"), lax.axis_index("tp")
    rows, width = hidden_acts.shape[0], w_down.shape[0]
    bits = [1 << b for b in range(nz.bit_length() - 1)]
    two = nx == 2

    cot = {0: cotangent}
    for bit in reversed(bits):
        for k in list(cot):
            cot[k ^ bit] = swap(cot[k], "fsdp", bit)
    hid = {}
    for k in range(nz):
        part = lax.dynamic_slice_in_dim(hidden_acts, (z ^ k) * width, width, 1)
        hid[k] = swap(part, "fsdp", k) if k else part

    basis = full_basis_of(projector)
    if two:
        w_mine, w_other = halves(w_down, 1, t)
        b_mine, b_other = halves(basis, 0, t)
        pairs = {k: ((cot[k], w_mine, b_mine), (swap(cot[k], "tp", 1), w_other, b_other)) for k in cot}
    else:
        pairs = {
            k: ((lax.all_gather(cot[k], "tp", axis=1, tiled=True), w_down, basis),) for k in cot
        }

    grads, coords = {}, {}
    for k in cot:
        back = sum(mm_t(c, w) for c, w, _ in pairs[k]).astype(bf16)
        grads[k] = swap(back, "fsdp", k) if k else back
        coords[k] = sum(mm(c, b) for c, _, b in pairs[k]).astype(bf16)
    order = jnp.stack([grads[k] for k in range(nz)])
    acts_grad = jnp.concatenate(
        [lax.dynamic_index_in_dim(order, z ^ j, 0, keepdims=False) for j in range(nz)], axis=1
    )

    outs = {}
    for k in range(nz):
        if two:
            away = mm(hid[k], w_other).astype(bf16)
            outs[k] = mm(hid[k], w_mine) + swap(away, "tp", 1).astype(f32)
        else:
            outs[k] = lax.psum_scatter(
                mm(hid[k], w_down).astype(bf16), "tp", scatter_dimension=1, tiled=True
            ).astype(f32)
    for bit in bits:
        for k in [k for k in outs if k & bit]:
            got = swap(outs.pop(k).astype(bf16), "fsdp", bit)
            outs[k ^ bit] = outs[k ^ bit] + got.astype(f32)
    block_out = outs[0].astype(bf16)

    all_hid = jnp.concatenate([hid[k] for k in range(nz)], axis=0)
    all_coords = jnp.concatenate([coords[k] for k in range(nz)], axis=0)
    local = mm_tn(all_hid, all_coords)
    owned = local + swap(local, "sub", 1)
    token_count = f32(rows * nz * lax.axis_size("sub"))
    direction, new_first, new_second = adam_rows(owned / token_count, first_moment, second_moment)
    weight_step = mm_t(direction, basis)
    return (block_out, acts_grad, weight_step, new_first, new_second)


light = pl.CostEstimate(flops=1, bytes_accessed=1, transcendentals=0)
strip = 512


def in_vmem(kernel, name, at, ins, outs, mib=12):
    vmem = pl.BlockSpec(memory_space=pltpu.VMEM)
    return pl.pallas_call(
        kernel,
        in_specs=[pl.BlockSpec(memory_space=pltpu.SMEM)] + [vmem] * len(ins),
        out_specs=[vmem] * len(outs),
        out_shape=outs,
        compiler_params=pltpu.CompilerParams(vmem_limit_bytes=mib << 20),
        cost_estimate=light,
        name=name,
    )(at, *ins)


def forward(at, h, w):
    rows, width = h.shape[0], w.shape[1]
    half = width // 2

    def kernel(at, h, w, p, m):
        mine, far = at[0] * half, (1 - at[0]) * half
        for j in range(0, half, strip):
            p[:, j : j + strip] = mm(h[...], w[:, pl.ds(pl.multiple_of(far + j, strip), strip)]).astype(bf16)
        for j in range(0, half, strip):
            m[:, j : j + strip] = mm(h[...], w[:, pl.ds(pl.multiple_of(mine + j, strip), strip)])

    return in_vmem(
        kernel, "forward", at, (h, w),
        [jax.ShapeDtypeStruct((rows, half), bf16), jax.ShapeDtypeStruct((rows, half), f32)],
    )


def backward(at, c, x, w, projector, got, shared):
    rows, half = c.shape
    units = w.shape[0]
    part = half // 2
    tall = 352

    def kernel(at, c, x, w, basis, got, shared, g, coords):
        mine = pl.multiple_of(at[0] * half, half)
        far = pl.multiple_of((1 - at[0]) * half, half)
        first = pl.multiple_of(at[1] * part, part)
        second = pl.multiple_of((1 - at[1]) * part, part)
        for j in range(0, units, tall):
            k = min(j + tall, units)
            g[j:k, :] = (
                mm_t(w[j:k, pl.ds(mine, half)], c[...]) + mm_t(w[j:k, pl.ds(far, half)], x[...])
            ).astype(bf16)
        coords[...] = (
            mm(c[...], basis[...])
            + mm(x[:, pl.ds(first, part)], got[...])
            + mm(x[:, pl.ds(second, part)], shared[...])
        ).astype(bf16)

    return in_vmem(
        kernel, "backward", at, (c, x, w, projector, got, shared),
        [
            jax.ShapeDtypeStruct((units, rows), bf16),
            jax.ShapeDtypeStruct((rows, projector.shape[1]), bf16),
        ],
    )


def project(at, hs, coords):
    n, units, rank = len(hs), hs[0].shape[1], coords[0].shape[1]
    tall = units // 2

    def kernel(at, *refs):
        upper, lower = refs[2 * n :]
        total = sum(mm_tn(h[...], c[...]) for h, c in zip(refs[:n], refs[n : 2 * n]))
        upper[...], lower[...] = total[:tall], total[tall:]

    return in_vmem(
        kernel, "project", at, (*hs, *coords), [jax.ShapeDtypeStruct((tall, rank), f32)] * 2
    )


def adam_step(at, here, there, tokens, first_moment, second_moment, projector, got, shared):
    units, rank = first_moment.shape
    half = projector.shape[0]
    part, width = half // 2, 2 * half
    tall = units // 4

    def kernel(at, h_up, h_low, t_up, t_low, first, second, basis, got, shared, step, new_first, new_second):
        upper = pl.program_id(0) < 2
        gradient = jnp.where(upper, h_up[...] + t_up[...], h_low[...] + t_low[...]) / f32(tokens)
        direction, new_first[...], new_second[...] = adam_rows(gradient, first[...], second[...])
        t, c = at[0], at[1]
        mine = pl.multiple_of(t * half, half)
        one = pl.multiple_of((1 - t) * half + c * part, part)
        two = pl.multiple_of((1 - t) * half + (1 - c) * part, part)
        step[:, pl.ds(mine, half)] = mm_t(direction, basis[...])
        step[:, pl.ds(one, part)] = mm_t(direction, got[...])
        step[:, pl.ds(two, part)] = mm_t(direction, shared[...])

    def block(index):
        return pl.BlockSpec((tall, rank), index)

    def up(i):
        return (jnp.minimum(i, 1), 0)

    def low(i):
        return (jnp.maximum(i, 2) - 2, 0)

    def row(i):
        return (i, 0)

    def whole(v):
        return pl.BlockSpec(v.shape, lambda i: (0, 0))

    small = jax.ShapeDtypeStruct((units, rank), f32)
    return pl.pallas_call(
        kernel,
        grid=(4,),
        in_specs=[pl.BlockSpec(memory_space=pltpu.SMEM)]
        + [block(up), block(low), block(up), block(low), block(row), block(row)]
        + [whole(projector), whole(got), whole(shared)],
        out_specs=[pl.BlockSpec((tall, width), row), block(row), block(row)],
        out_shape=[jax.ShapeDtypeStruct((units, width), f32), small, small],
        compiler_params=pltpu.CompilerParams(vmem_limit_bytes=24 << 20),
        cost_estimate=light,
        name="adam_step",
    )(at, *here, *there, first_moment, second_moment, projector, got, shared)


class Order:
    def __init__(self):
        self.last = ()

    def go(self, x):
        return lax.optimization_barrier((x, *self.last))[0]

    def seen(self, *done):
        self.last = done


def shards_line(hidden_acts, cotangent, w_down, projector, first_moment, second_moment):
    z, t, c = lax.axis_index("fsdp"), lax.axis_index("tp"), lax.axis_index("sub")
    rows, width = hidden_acts.shape[0], w_down.shape[0]
    at = jnp.stack([t, c]).astype(jnp.int32)
    tokens = rows * lax.axis_size("fsdp") * lax.axis_size("sub")
    order = Order()
    go, seen = order.go, order.seen

    def own_units(k):
        return lax.dynamic_slice_in_dim(hidden_acts, (z ^ k) * width, width, 1)

    c0 = cotangent
    c2 = swap(c0, "fsdp", 2, "c2")
    c1 = swap(c0, "fsdp", 1, "c1")
    x0 = swap(c0, "tp", 1, "x0")
    h0, h1, h2, h3 = (own_units(k) for k in range(4))
    seen(h0)
    half = swap(halves(go(projector), 0, c)[0], "tp", 1, "half")
    p0, m0 = forward(at, h0, w_down)
    seen(p0, c2, half, c1, x0)
    x2 = swap(go(c2), "tp", 1, "x2")
    h3 = swap(go(h3), "fsdp", 3, "h3")
    c3 = swap(go(c2), "fsdp", 1, "c3")
    basis = swap(go(half), "sub", 1, "basis")
    seen(p0, c1, x0, basis)
    x1 = swap(go(c1), "tp", 1, "x1")
    g0, k0 = backward(at, go(c0), x0, w_down, projector, half, basis)
    seen(g0, x2)
    g2, k2 = backward(at, go(c2), x2, w_down, projector, half, basis)
    seen(g2, h3)
    h2 = swap(go(h2), "fsdp", 2, "h2")
    h1 = swap(go(h1), "fsdp", 1, "h1")
    p3, m3 = forward(at, go(h3), w_down)
    seen(p3, c3)
    x3 = swap(go(c3), "tp", 1, "x3")
    seen(p3, c3, x1)
    g1, k1 = backward(at, go(c1), x1, w_down, projector, half, basis)
    seen(g1, h2)
    y3 = swap(go(p3), "tp", 1, "y3")
    a2 = swap(go(g2), "fsdp", 2, "a2")
    p2, m2 = forward(at, go(h2), w_down)
    seen(p2, h1)
    a1 = swap(go(g1), "fsdp", 1, "a1")
    p1, m1 = forward(at, go(h1), w_down)
    seen(p1, x3)
    y2 = swap(go(p2), "tp", 1, "y2")
    g3, k3 = backward(at, go(c3), x3, w_down, projector, half, basis)
    a3 = swap(g3, "fsdp", 3, "a3")
    seen(g3, y3, a2, a1)
    o3 = (go(m3) + y3.astype(f32)).astype(bf16)
    r3 = swap(o3, "fsdp", 1, "r3")
    y1 = swap(go(p1), "tp", 1, "y1")
    seen(o3)
    local = project(at, (h0, h1, h2, h3), (go(k0), k1, k2, k3))
    other = [swap(v, "sub", 1, "rows") for v in local]
    seen(local[0], y2, r3)
    o2 = (go(m2) + y2.astype(f32) + r3.astype(f32)).astype(bf16)
    r2 = swap(o2, "fsdp", 2, "r2")
    y0 = swap(go(p0), "tp", 1, "y0")
    seen(o2, a3)
    by_owner = jnp.stack([go(g0), a1, a2, a3])
    acts_grad = jnp.concatenate(
        [lax.dynamic_index_in_dim(by_owner, z ^ j, 0, keepdims=False) for j in range(4)], axis=0
    ).T
    seen(o2, acts_grad, y1)
    o1 = (go(m1) + y1.astype(f32)).astype(bf16)
    r1 = swap(o1, "fsdp", 1, "r1")
    seen(o1)
    weight_step, new_first, new_second = adam_step(
        at, local, (go(other[0]), other[1]), tokens, first_moment, second_moment, projector, half, basis
    )
    seen(weight_step)
    block_out = (
        go(m0) + y0.astype(f32) + r1.astype(f32) + r2.astype(f32)
    ).astype(bf16)
    return (block_out, acts_grad, weight_step, new_first, new_second)


def solution(mesh):
    in_specs = (
        P(("groups", "fsdp", "sub"), "tp"),
        P(("groups", "fsdp", "sub"), "tp"),
        P(("tp", "fsdp"), None),
        P("tp", None),
        P(("groups", "tp", "fsdp"), None),
        P(("groups", "tp", "fsdp"), None),
    )
    out_specs = (
        P(("groups", "fsdp", "sub"), "tp"),
        P(("groups", "fsdp", "sub"), "tp"),
        P(("groups", "tp", "fsdp"), None),
        P(("groups", "tp", "fsdp"), None),
        P(("groups", "tp", "fsdp"), None),
    )
    line = mesh.shape["fsdp"] == 4 and mesh.shape["tp"] == 2
    shards = shards_line if line else shards_any
    return jax.shard_map(shards, mesh=mesh, in_specs=in_specs, out_specs=out_specs, check_vma=False)
```

```python
import jax
import jax.numpy as jnp
from jax import lax
from jax.experimental import pallas as pl
from jax.experimental.pallas import tpu as pltpu
from jax.sharding import PartitionSpec as P

first_decay = 0.9
second_decay = 0.999
first_fix = 1.0 - 0.9**10
second_fix = 1.0 - 0.999**10
epsilon = 1e-08

f32 = jnp.float32
bf16 = jnp.bfloat16


def swap(x, axis, bit, name="swap"):
    n = lax.axis_size(axis)
    with jax.named_scope(name):
        return lax.ppermute(x, axis, [(i, i ^ bit) for i in range(n)])


def mm(a, b):
    return jnp.dot(a, b, preferred_element_type=f32)


def mm_t(a, b):
    return lax.dot_general(a, b, (((1,), (1,)), ((), ())), preferred_element_type=f32)


def mm_tn(a, b):
    return lax.dot_general(a, b, (((0,), (0,)), ((), ())), preferred_element_type=f32)


def adam_rows(gradient, first_rows, second_rows):
    new_first = first_decay * first_rows + (1.0 - first_decay) * gradient
    new_second = second_decay * second_rows + (1.0 - second_decay) * gradient * gradient
    direction = (new_first / first_fix / (jnp.sqrt(new_second / second_fix) + epsilon)).astype(bf16)
    return direction, new_first, new_second


def halves(x, axis, t):
    n = x.shape[axis] // 2
    return (
        lax.dynamic_slice_in_dim(x, t * n, n, axis),
        lax.dynamic_slice_in_dim(x, (1 - t) * n, n, axis),
    )


def in_order(mine, other, index, axis):
    return jnp.concatenate(
        [jnp.where(index == 0, mine, other), jnp.where(index == 0, other, mine)], axis=axis
    )


def full_basis_of(projector):
    if lax.axis_size("tp") != 2:
        return lax.all_gather(projector, "tp", axis=0, tiled=True)
    t, c = lax.axis_index("tp"), lax.axis_index("sub")
    mine = halves(projector, 0, c)[0]
    got = swap(mine, "tp", 1)
    other = in_order(got, swap(got, "sub", 1), c, 0)
    return in_order(projector, other, t, 0)


def shards_any(hidden_acts, cotangent, w_down, projector, first_moment, second_moment):
    nz, nx = lax.axis_size("fsdp"), lax.axis_size("tp")
    z, t = lax.axis_index("fsdp"), lax.axis_index("tp")
    rows, width = hidden_acts.shape[0], w_down.shape[0]
    bits = [1 << b for b in range(nz.bit_length() - 1)]
    two = nx == 2

    cot = {0: cotangent}
    for bit in reversed(bits):
        for k in list(cot):
            cot[k ^ bit] = swap(cot[k], "fsdp", bit)
    hid = {}
    for k in range(nz):
        part = lax.dynamic_slice_in_dim(hidden_acts, (z ^ k) * width, width, 1)
        hid[k] = swap(part, "fsdp", k) if k else part

    basis = full_basis_of(projector)
    if two:
        w_mine, w_other = halves(w_down, 1, t)
        b_mine, b_other = halves(basis, 0, t)
        pairs = {k: ((cot[k], w_mine, b_mine), (swap(cot[k], "tp", 1), w_other, b_other)) for k in cot}
    else:
        pairs = {
            k: ((lax.all_gather(cot[k], "tp", axis=1, tiled=True), w_down, basis),) for k in cot
        }

    grads, coords = {}, {}
    for k in cot:
        back = sum(mm_t(c, w) for c, w, _ in pairs[k]).astype(bf16)
        grads[k] = swap(back, "fsdp", k) if k else back
        coords[k] = sum(mm(c, b) for c, _, b in pairs[k]).astype(bf16)
    order = jnp.stack([grads[k] for k in range(nz)])
    acts_grad = jnp.concatenate(
        [lax.dynamic_index_in_dim(order, z ^ j, 0, keepdims=False) for j in range(nz)], axis=1
    )

    outs = {}
    for k in range(nz):
        if two:
            away = mm(hid[k], w_other).astype(bf16)
            outs[k] = mm(hid[k], w_mine) + swap(away, "tp", 1).astype(f32)
        else:
            outs[k] = lax.psum_scatter(
                mm(hid[k], w_down).astype(bf16), "tp", scatter_dimension=1, tiled=True
            ).astype(f32)
    for bit in bits:
        for k in [k for k in outs if k & bit]:
            got = swap(outs.pop(k).astype(bf16), "fsdp", bit)
            outs[k ^ bit] = outs[k ^ bit] + got.astype(f32)
    block_out = outs[0].astype(bf16)

    all_hid = jnp.concatenate([hid[k] for k in range(nz)], axis=0)
    all_coords = jnp.concatenate([coords[k] for k in range(nz)], axis=0)
    local = mm_tn(all_hid, all_coords)
    owned = local + swap(local, "sub", 1)
    token_count = f32(rows * nz * lax.axis_size("sub"))
    direction, new_first, new_second = adam_rows(owned / token_count, first_moment, second_moment)
    weight_step = mm_t(direction, basis)
    return (block_out, acts_grad, weight_step, new_first, new_second)


light = pl.CostEstimate(flops=1, bytes_accessed=1, transcendentals=0)
strip = 512


def in_vmem(kernel, name, at, ins, outs, mib=12):
    vmem = pl.BlockSpec(memory_space=pltpu.VMEM)
    return pl.pallas_call(
        kernel,
        in_specs=[pl.BlockSpec(memory_space=pltpu.SMEM)] + [vmem] * len(ins),
        out_specs=[vmem] * len(outs),
        out_shape=outs,
        compiler_params=pltpu.CompilerParams(vmem_limit_bytes=mib << 20),
        cost_estimate=light,
        name=name,
    )(at, *ins)


def forward(at, h, w):
    rows, width = h.shape[0], w.shape[1]
    half = width // 2

    def kernel(at, h, w, p, m):
        mine, far = at[0] * half, (1 - at[0]) * half
        for j in range(0, half, strip):
            p[:, j : j + strip] = mm(h[...], w[:, pl.ds(pl.multiple_of(far + j, strip), strip)]).astype(bf16)
        for j in range(0, half, strip):
            m[:, j : j + strip] = mm(h[...], w[:, pl.ds(pl.multiple_of(mine + j, strip), strip)])

    return in_vmem(
        kernel, "forward", at, (h, w),
        [jax.ShapeDtypeStruct((rows, half), bf16), jax.ShapeDtypeStruct((rows, half), f32)],
    )


def backward(at, c, x, w, projector, got, shared):
    rows, half = c.shape
    units = w.shape[0]
    part = half // 2
    tall = 352

    def kernel(at, c, x, w, basis, got, shared, g, coords):
        mine = pl.multiple_of(at[0] * half, half)
        far = pl.multiple_of((1 - at[0]) * half, half)
        first = pl.multiple_of(at[1] * part, part)
        second = pl.multiple_of((1 - at[1]) * part, part)
        for j in range(0, units, tall):
            k = min(j + tall, units)
            g[j:k, :] = (
                mm_t(w[j:k, pl.ds(mine, half)], c[...]) + mm_t(w[j:k, pl.ds(far, half)], x[...])
            ).astype(bf16)
        coords[...] = (
            mm(c[...], basis[...])
            + mm(x[:, pl.ds(first, part)], got[...])
            + mm(x[:, pl.ds(second, part)], shared[...])
        ).astype(bf16)

    return in_vmem(
        kernel, "backward", at, (c, x, w, projector, got, shared),
        [
            jax.ShapeDtypeStruct((units, rows), bf16),
            jax.ShapeDtypeStruct((rows, projector.shape[1]), bf16),
        ],
    )


def project(at, hs, coords):
    n, units, rank = len(hs), hs[0].shape[1], coords[0].shape[1]
    tall = units // 2

    def kernel(at, *refs):
        upper, lower = refs[2 * n :]
        total = sum(mm_tn(h[...], c[...]) for h, c in zip(refs[:n], refs[n : 2 * n]))
        upper[...], lower[...] = total[:tall], total[tall:]

    return in_vmem(
        kernel, "project", at, (*hs, *coords), [jax.ShapeDtypeStruct((tall, rank), f32)] * 2
    )


def adam_step(at, here, there, tokens, first_moment, second_moment, projector, got, shared):
    units, rank = first_moment.shape
    half = projector.shape[0]
    part, width = half // 2, 2 * half
    tall = units // 4

    def kernel(at, h_up, h_low, t_up, t_low, first, second, basis, got, shared, step, new_first, new_second):
        upper = pl.program_id(0) < 2
        gradient = jnp.where(upper, h_up[...] + t_up[...], h_low[...] + t_low[...]) / f32(tokens)
        direction, new_first[...], new_second[...] = adam_rows(gradient, first[...], second[...])
        t, c = at[0], at[1]
        mine = pl.multiple_of(t * half, half)
        one = pl.multiple_of((1 - t) * half + c * part, part)
        two = pl.multiple_of((1 - t) * half + (1 - c) * part, part)
        step[:, pl.ds(mine, half)] = mm_t(direction, basis[...])
        step[:, pl.ds(one, part)] = mm_t(direction, got[...])
        step[:, pl.ds(two, part)] = mm_t(direction, shared[...])

    def block(index):
        return pl.BlockSpec((tall, rank), index)

    def up(i):
        return (jnp.minimum(i, 1), 0)

    def low(i):
        return (jnp.maximum(i, 2) - 2, 0)

    def row(i):
        return (i, 0)

    def whole(v):
        return pl.BlockSpec(v.shape, lambda i: (0, 0))

    small = jax.ShapeDtypeStruct((units, rank), f32)
    return pl.pallas_call(
        kernel,
        grid=(4,),
        in_specs=[pl.BlockSpec(memory_space=pltpu.SMEM)]
        + [block(up), block(low), block(up), block(low), block(row), block(row)]
        + [whole(projector), whole(got), whole(shared)],
        out_specs=[pl.BlockSpec((tall, width), row), block(row), block(row)],
        out_shape=[jax.ShapeDtypeStruct((units, width), f32), small, small],
        compiler_params=pltpu.CompilerParams(vmem_limit_bytes=24 << 20),
        cost_estimate=light,
        name="adam_step",
    )(at, *here, *there, first_moment, second_moment, projector, got, shared)


class Order:
    def __init__(self):
        self.last = ()

    def go(self, x):
        return lax.optimization_barrier((x, *self.last))[0]

    def seen(self, *done):
        self.last = done


def shards_line(hidden_acts, cotangent, w_down, projector, first_moment, second_moment):
    z, t, c = lax.axis_index("fsdp"), lax.axis_index("tp"), lax.axis_index("sub")
    rows, width = hidden_acts.shape[0], w_down.shape[0]
    at = jnp.stack([t, c]).astype(jnp.int32)
    tokens = rows * lax.axis_size("fsdp") * lax.axis_size("sub")
    order = Order()
    go, seen = order.go, order.seen

    def own_units(k):
        return lax.dynamic_slice_in_dim(hidden_acts, (z ^ k) * width, width, 1)

    c0 = cotangent
    c2 = swap(c0, "fsdp", 2, "c2")
    c1 = swap(c0, "fsdp", 1, "c1")
    x0 = swap(c0, "tp", 1, "x0")
    h0, h1, h2, h3 = (own_units(k) for k in range(4))
    seen(h0)
    half = swap(halves(go(projector), 0, c)[0], "tp", 1, "half")
    p0, m0 = forward(at, h0, w_down)
    seen(p0, c2, half, c1, x0)
    x2 = swap(go(c2), "tp", 1, "x2")
    h3 = swap(go(h3), "fsdp", 3, "h3")
    c3 = swap(go(c2), "fsdp", 1, "c3")
    basis = swap(go(half), "sub", 1, "basis")
    seen(p0, c1, x0, basis)
    x1 = swap(go(c1), "tp", 1, "x1")
    g0, k0 = backward(at, go(c0), x0, w_down, projector, half, basis)
    seen(g0, x2)
    g2, k2 = backward(at, go(c2), x2, w_down, projector, half, basis)
    seen(g2, h3)
    h2 = swap(go(h2), "fsdp", 2, "h2")
    h1 = swap(go(h1), "fsdp", 1, "h1")
    p3, m3 = forward(at, go(h3), w_down)
    seen(p3, c3)
    x3 = swap(go(c3), "tp", 1, "x3")
    seen(p3, c3, x1)
    g1, k1 = backward(at, go(c1), x1, w_down, projector, half, basis)
    seen(g1, h2)
    y3 = swap(go(p3), "tp", 1, "y3")
    a2 = swap(go(g2), "fsdp", 2, "a2")
    p2, m2 = forward(at, go(h2), w_down)
    seen(p2, h1)
    a1 = swap(go(g1), "fsdp", 1, "a1")
    p1, m1 = forward(at, go(h1), w_down)
    seen(p1, x3)
    y2 = swap(go(p2), "tp", 1, "y2")
    g3, k3 = backward(at, go(c3), x3, w_down, projector, half, basis)
    a3 = swap(g3, "fsdp", 3, "a3")
    seen(g3, y3, a2, a1)
    o3 = (go(m3) + y3.astype(f32)).astype(bf16)
    r3 = swap(o3, "fsdp", 1, "r3")
    y1 = swap(go(p1), "tp", 1, "y1")
    seen(o3)
    local = project(at, (h0, h1, h2, h3), (go(k0), k1, k2, k3))
    other = [swap(v, "sub", 1, "rows") for v in local]
    seen(local[0], y1, y2)
    o1 = (go(m1) + y1.astype(f32)).astype(bf16)
    r1 = swap(o1, "fsdp", 1, "r1")
    seen(o1, r3)
    o2 = (go(m2) + y2.astype(f32) + r3.astype(f32)).astype(bf16)
    r2 = swap(o2, "fsdp", 2, "r2")
    y0 = swap(go(p0), "tp", 1, "y0")
    seen(o2, a3)
    by_owner = jnp.stack([go(g0), a1, a2, a3])
    acts_grad = jnp.concatenate(
        [lax.dynamic_index_in_dim(by_owner, z ^ j, 0, keepdims=False) for j in range(4)], axis=0
    ).T
    seen(acts_grad)
    weight_step, new_first, new_second = adam_step(
        at, local, (go(other[0]), other[1]), tokens, first_moment, second_moment, projector, half, basis
    )
    seen(weight_step)
    block_out = (
        go(m0) + y0.astype(f32) + r1.astype(f32) + r2.astype(f32)
    ).astype(bf16)
    return (block_out, acts_grad, weight_step, new_first, new_second)


def solution(mesh):
    in_specs = (
        P(("groups", "fsdp", "sub"), "tp"),
        P(("groups", "fsdp", "sub"), "tp"),
        P(("tp", "fsdp"), None),
        P("tp", None),
        P(("groups", "tp", "fsdp"), None),
        P(("groups", "tp", "fsdp"), None),
    )
    out_specs = (
        P(("groups", "fsdp", "sub"), "tp"),
        P(("groups", "fsdp", "sub"), "tp"),
        P(("groups", "tp", "fsdp"), None),
        P(("groups", "tp", "fsdp"), None),
        P(("groups", "tp", "fsdp"), None),
    )
    line = mesh.shape["fsdp"] == 4 and mesh.shape["tp"] == 2
    shards = shards_line if line else shards_any
    return jax.shard_map(shards, mesh=mesh, in_specs=in_specs, out_specs=out_specs, check_vma=False)
```

```python
import jax
import jax.numpy as jnp
from jax import lax
from jax.experimental import pallas as pl
from jax.experimental.pallas import tpu as pltpu
from jax.sharding import PartitionSpec as P

first_decay = 0.9
second_decay = 0.999
first_fix = 1.0 - 0.9**10
second_fix = 1.0 - 0.999**10
epsilon = 1e-08

f32 = jnp.float32
bf16 = jnp.bfloat16


def swap(x, axis, bit, name="swap"):
    n = lax.axis_size(axis)
    with jax.named_scope(name):
        return lax.ppermute(x, axis, [(i, i ^ bit) for i in range(n)])


def mm(a, b):
    return jnp.dot(a, b, preferred_element_type=f32)


def mm_t(a, b):
    return lax.dot_general(a, b, (((1,), (1,)), ((), ())), preferred_element_type=f32)


def mm_tn(a, b):
    return lax.dot_general(a, b, (((0,), (0,)), ((), ())), preferred_element_type=f32)


def adam_rows(gradient, first_rows, second_rows):
    new_first = first_decay * first_rows + (1.0 - first_decay) * gradient
    new_second = second_decay * second_rows + (1.0 - second_decay) * gradient * gradient
    direction = (new_first / first_fix / (jnp.sqrt(new_second / second_fix) + epsilon)).astype(bf16)
    return direction, new_first, new_second


def halves(x, axis, t):
    n = x.shape[axis] // 2
    return (
        lax.dynamic_slice_in_dim(x, t * n, n, axis),
        lax.dynamic_slice_in_dim(x, (1 - t) * n, n, axis),
    )


def in_order(mine, other, index, axis):
    return jnp.concatenate(
        [jnp.where(index == 0, mine, other), jnp.where(index == 0, other, mine)], axis=axis
    )


def full_basis_of(projector):
    if lax.axis_size("tp") != 2:
        return lax.all_gather(projector, "tp", axis=0, tiled=True)
    t, c = lax.axis_index("tp"), lax.axis_index("sub")
    mine = halves(projector, 0, c)[0]
    got = swap(mine, "tp", 1)
    other = in_order(got, swap(got, "sub", 1), c, 0)
    return in_order(projector, other, t, 0)


def shards_any(hidden_acts, cotangent, w_down, projector, first_moment, second_moment):
    nz, nx = lax.axis_size("fsdp"), lax.axis_size("tp")
    z, t = lax.axis_index("fsdp"), lax.axis_index("tp")
    rows, width = hidden_acts.shape[0], w_down.shape[0]
    bits = [1 << b for b in range(nz.bit_length() - 1)]
    two = nx == 2

    cot = {0: cotangent}
    for bit in reversed(bits):
        for k in list(cot):
            cot[k ^ bit] = swap(cot[k], "fsdp", bit)
    hid = {}
    for k in range(nz):
        part = lax.dynamic_slice_in_dim(hidden_acts, (z ^ k) * width, width, 1)
        hid[k] = swap(part, "fsdp", k) if k else part

    basis = full_basis_of(projector)
    if two:
        w_mine, w_other = halves(w_down, 1, t)
        b_mine, b_other = halves(basis, 0, t)
        pairs = {k: ((cot[k], w_mine, b_mine), (swap(cot[k], "tp", 1), w_other, b_other)) for k in cot}
    else:
        pairs = {
            k: ((lax.all_gather(cot[k], "tp", axis=1, tiled=True), w_down, basis),) for k in cot
        }

    grads, coords = {}, {}
    for k in cot:
        back = sum(mm_t(c, w) for c, w, _ in pairs[k]).astype(bf16)
        grads[k] = swap(back, "fsdp", k) if k else back
        coords[k] = sum(mm(c, b) for c, _, b in pairs[k]).astype(bf16)
    order = jnp.stack([grads[k] for k in range(nz)])
    acts_grad = jnp.concatenate(
        [lax.dynamic_index_in_dim(order, z ^ j, 0, keepdims=False) for j in range(nz)], axis=1
    )

    outs = {}
    for k in range(nz):
        if two:
            away = mm(hid[k], w_other).astype(bf16)
            outs[k] = mm(hid[k], w_mine) + swap(away, "tp", 1).astype(f32)
        else:
            outs[k] = lax.psum_scatter(
                mm(hid[k], w_down).astype(bf16), "tp", scatter_dimension=1, tiled=True
            ).astype(f32)
    for bit in bits:
        for k in [k for k in outs if k & bit]:
            got = swap(outs.pop(k).astype(bf16), "fsdp", bit)
            outs[k ^ bit] = outs[k ^ bit] + got.astype(f32)
    block_out = outs[0].astype(bf16)

    all_hid = jnp.concatenate([hid[k] for k in range(nz)], axis=0)
    all_coords = jnp.concatenate([coords[k] for k in range(nz)], axis=0)
    local = mm_tn(all_hid, all_coords)
    owned = local + swap(local, "sub", 1)
    token_count = f32(rows * nz * lax.axis_size("sub"))
    direction, new_first, new_second = adam_rows(owned / token_count, first_moment, second_moment)
    weight_step = mm_t(direction, basis)
    return (block_out, acts_grad, weight_step, new_first, new_second)


light = pl.CostEstimate(flops=1, bytes_accessed=1, transcendentals=0)
strip = 512


def in_vmem(kernel, name, at, ins, outs, mib=12):
    vmem = pl.BlockSpec(memory_space=pltpu.VMEM)
    return pl.pallas_call(
        kernel,
        in_specs=[pl.BlockSpec(memory_space=pltpu.SMEM)] + [vmem] * len(ins),
        out_specs=[vmem] * len(outs),
        out_shape=outs,
        compiler_params=pltpu.CompilerParams(vmem_limit_bytes=mib << 20),
        cost_estimate=light,
        name=name,
    )(at, *ins)


def forward(at, h, w):
    rows, width = h.shape[0], w.shape[1]
    half = width // 2

    def kernel(at, h, w, p, m):
        mine, far = at[0] * half, (1 - at[0]) * half
        for j in range(0, half, strip):
            p[:, j : j + strip] = mm(h[...], w[:, pl.ds(pl.multiple_of(far + j, strip), strip)]).astype(bf16)
        for j in range(0, half, strip):
            m[:, j : j + strip] = mm(h[...], w[:, pl.ds(pl.multiple_of(mine + j, strip), strip)])

    return in_vmem(
        kernel, "forward", at, (h, w),
        [jax.ShapeDtypeStruct((rows, half), bf16), jax.ShapeDtypeStruct((rows, half), f32)],
    )


def backward(at, c, x, w, projector, got, shared):
    rows, half = c.shape
    units = w.shape[0]
    part = half // 2
    tall = 352

    def kernel(at, c, x, w, basis, got, shared, g, coords):
        mine = pl.multiple_of(at[0] * half, half)
        far = pl.multiple_of((1 - at[0]) * half, half)
        first = pl.multiple_of(at[1] * part, part)
        second = pl.multiple_of((1 - at[1]) * part, part)
        for j in range(0, units, tall):
            k = min(j + tall, units)
            g[j:k, :] = (
                mm_t(w[j:k, pl.ds(mine, half)], c[...]) + mm_t(w[j:k, pl.ds(far, half)], x[...])
            ).astype(bf16)
        coords[...] = (
            mm(c[...], basis[...])
            + mm(x[:, pl.ds(first, part)], got[...])
            + mm(x[:, pl.ds(second, part)], shared[...])
        ).astype(bf16)

    return in_vmem(
        kernel, "backward", at, (c, x, w, projector, got, shared),
        [
            jax.ShapeDtypeStruct((units, rows), bf16),
            jax.ShapeDtypeStruct((rows, projector.shape[1]), bf16),
        ],
    )


def project(at, hs, coords):
    n, units, rank = len(hs), hs[0].shape[1], coords[0].shape[1]
    tall = units // 2

    def kernel(at, *refs):
        upper, lower = refs[2 * n :]
        total = sum(mm_tn(h[...], c[...]) for h, c in zip(refs[:n], refs[n : 2 * n]))
        upper[...], lower[...] = total[:tall], total[tall:]

    return in_vmem(
        kernel, "project", at, (*hs, *coords), [jax.ShapeDtypeStruct((tall, rank), f32)] * 2
    )


def adam_step(at, here, there, tokens, first_moment, second_moment, projector, got, shared):
    units, rank = first_moment.shape
    half = projector.shape[0]
    part, width = half // 2, 2 * half
    tall = units // 4

    def kernel(at, h_up, h_low, t_up, t_low, first, second, basis, got, shared, step, new_first, new_second):
        upper = pl.program_id(0) < 2
        gradient = jnp.where(upper, h_up[...] + t_up[...], h_low[...] + t_low[...]) / f32(tokens)
        direction, new_first[...], new_second[...] = adam_rows(gradient, first[...], second[...])
        t, c = at[0], at[1]
        mine = pl.multiple_of(t * half, half)
        one = pl.multiple_of((1 - t) * half + c * part, part)
        two = pl.multiple_of((1 - t) * half + (1 - c) * part, part)
        step[:, pl.ds(mine, half)] = mm_t(direction, basis[...])
        step[:, pl.ds(one, part)] = mm_t(direction, got[...])
        step[:, pl.ds(two, part)] = mm_t(direction, shared[...])

    def block(index):
        return pl.BlockSpec((tall, rank), index)

    def up(i):
        return (jnp.minimum(i, 1), 0)

    def low(i):
        return (jnp.maximum(i, 2) - 2, 0)

    def row(i):
        return (i, 0)

    def whole(v):
        return pl.BlockSpec(v.shape, lambda i: (0, 0))

    small = jax.ShapeDtypeStruct((units, rank), f32)
    return pl.pallas_call(
        kernel,
        grid=(4,),
        in_specs=[pl.BlockSpec(memory_space=pltpu.SMEM)]
        + [block(up), block(low), block(up), block(low), block(row), block(row)]
        + [whole(projector), whole(got), whole(shared)],
        out_specs=[pl.BlockSpec((tall, width), row), block(row), block(row)],
        out_shape=[jax.ShapeDtypeStruct((units, width), f32), small, small],
        compiler_params=pltpu.CompilerParams(vmem_limit_bytes=24 << 20),
        cost_estimate=light,
        name="adam_step",
    )(at, *here, *there, first_moment, second_moment, projector, got, shared)


class Order:
    def __init__(self):
        self.last = ()

    def go(self, x):
        return lax.optimization_barrier((x, *self.last))[0]

    def seen(self, *done):
        self.last = done


def shards_line(hidden_acts, cotangent, w_down, projector, first_moment, second_moment):
    z, t, c = lax.axis_index("fsdp"), lax.axis_index("tp"), lax.axis_index("sub")
    rows, width = hidden_acts.shape[0], w_down.shape[0]
    at = jnp.stack([t, c]).astype(jnp.int32)
    tokens = rows * lax.axis_size("fsdp") * lax.axis_size("sub")
    order = Order()
    go, seen = order.go, order.seen

    def own_units(k):
        return lax.dynamic_slice_in_dim(hidden_acts, (z ^ k) * width, width, 1)

    c0 = cotangent
    c2 = swap(c0, "fsdp", 2, "c2")
    x0 = swap(c0, "tp", 1, "x0")
    h0, h1, h2, h3 = (own_units(k) for k in range(4))
    seen(h0)
    c1 = swap(go(c0), "fsdp", 1, "c1")
    half = swap(halves(go(projector), 0, c)[0], "tp", 1, "half")
    p0, m0 = forward(at, h0, w_down)
    seen(p0, c2, half, x0)
    x2 = swap(go(c2), "tp", 1, "x2")
    h3 = swap(go(h3), "fsdp", 3, "h3")
    c3 = swap(go(c2), "fsdp", 1, "c3")
    basis = swap(go(half), "sub", 1, "basis")
    seen(p0, c1, x0, basis)
    x1 = swap(go(c1), "tp", 1, "x1")
    g0, k0 = backward(at, go(c0), x0, w_down, projector, half, basis)
    seen(g0, x2)
    g2, k2 = backward(at, go(c2), x2, w_down, projector, half, basis)
    seen(g2, h3)
    h2 = swap(go(h2), "fsdp", 2, "h2")
    h1 = swap(go(h1), "fsdp", 1, "h1")
    p3, m3 = forward(at, go(h3), w_down)
    seen(p3, c3)
    x3 = swap(go(c3), "tp", 1, "x3")
    seen(p3, c3, x1)
    g1, k1 = backward(at, go(c1), x1, w_down, projector, half, basis)
    seen(g1, h2)
    y3 = swap(go(p3), "tp", 1, "y3")
    a2 = swap(go(g2), "fsdp", 2, "a2")
    p2, m2 = forward(at, go(h2), w_down)
    seen(p2, h1)
    a1 = swap(go(g1), "fsdp", 1, "a1")
    p1, m1 = forward(at, go(h1), w_down)
    seen(p1, x3)
    y2 = swap(go(p2), "tp", 1, "y2")
    g3, k3 = backward(at, go(c3), x3, w_down, projector, half, basis)
    a3 = swap(g3, "fsdp", 3, "a3")
    seen(g3, y3, a2, a1)
    o3 = (go(m3) + y3.astype(f32)).astype(bf16)
    r3 = swap(o3, "fsdp", 1, "r3")
    y1 = swap(go(p1), "tp", 1, "y1")
    seen(o3)
    local = project(at, (h0, h1, h2, h3), (go(k0), k1, k2, k3))
    other = [swap(v, "sub", 1, "rows") for v in local]
    seen(local[0], y1, y2)
    o1 = (go(m1) + y1.astype(f32)).astype(bf16)
    r1 = swap(o1, "fsdp", 1, "r1")
    seen(o1, r3)
    o2 = (go(m2) + y2.astype(f32) + r3.astype(f32)).astype(bf16)
    r2 = swap(o2, "fsdp", 2, "r2")
    y0 = swap(go(p0), "tp", 1, "y0")
    seen(o2, a3)
    by_owner = jnp.stack([go(g0), a1, a2, a3])
    acts_grad = jnp.concatenate(
        [lax.dynamic_index_in_dim(by_owner, z ^ j, 0, keepdims=False) for j in range(4)], axis=0
    ).T
    seen(acts_grad)
    weight_step, new_first, new_second = adam_step(
        at, local, (go(other[0]), other[1]), tokens, first_moment, second_moment, projector, half, basis
    )
    seen(weight_step)
    o0 = go(m0) + y0.astype(f32) + r1.astype(f32)
    seen(o0)
    block_out = (o0 + go(r2).astype(f32)).astype(bf16)
    return (block_out, acts_grad, weight_step, new_first, new_second)


def solution(mesh):
    in_specs = (
        P(("groups", "fsdp", "sub"), "tp"),
        P(("groups", "fsdp", "sub"), "tp"),
        P(("tp", "fsdp"), None),
        P("tp", None),
        P(("groups", "tp", "fsdp"), None),
        P(("groups", "tp", "fsdp"), None),
    )
    out_specs = (
        P(("groups", "fsdp", "sub"), "tp"),
        P(("groups", "fsdp", "sub"), "tp"),
        P(("groups", "tp", "fsdp"), None),
        P(("groups", "tp", "fsdp"), None),
        P(("groups", "tp", "fsdp"), None),
    )
    line = mesh.shape["fsdp"] == 4 and mesh.shape["tp"] == 2
    shards = shards_line if line else shards_any
    return jax.shard_map(shards, mesh=mesh, in_specs=in_specs, out_specs=out_specs, check_vma=False)
```

```python
import jax
import jax.numpy as jnp
from jax import lax
from jax.experimental import pallas as pl
from jax.experimental.pallas import tpu as pltpu
from jax.sharding import PartitionSpec as P

first_decay = 0.9
second_decay = 0.999
first_fix = 1.0 - 0.9**10
second_fix = 1.0 - 0.999**10
epsilon = 1e-08

f32 = jnp.float32
bf16 = jnp.bfloat16


def swap(x, axis, bit, name="swap"):
    n = lax.axis_size(axis)
    with jax.named_scope(name):
        return lax.ppermute(x, axis, [(i, i ^ bit) for i in range(n)])


def mm(a, b):
    return jnp.dot(a, b, preferred_element_type=f32)


def mm_t(a, b):
    return lax.dot_general(a, b, (((1,), (1,)), ((), ())), preferred_element_type=f32)


def mm_tn(a, b):
    return lax.dot_general(a, b, (((0,), (0,)), ((), ())), preferred_element_type=f32)


def adam_rows(gradient, first_rows, second_rows):
    new_first = first_decay * first_rows + (1.0 - first_decay) * gradient
    new_second = second_decay * second_rows + (1.0 - second_decay) * gradient * gradient
    direction = (new_first / first_fix / (jnp.sqrt(new_second / second_fix) + epsilon)).astype(bf16)
    return direction, new_first, new_second


def halves(x, axis, t):
    n = x.shape[axis] // 2
    return (
        lax.dynamic_slice_in_dim(x, t * n, n, axis),
        lax.dynamic_slice_in_dim(x, (1 - t) * n, n, axis),
    )


def in_order(mine, other, index, axis):
    return jnp.concatenate(
        [jnp.where(index == 0, mine, other), jnp.where(index == 0, other, mine)], axis=axis
    )


def full_basis_of(projector):
    if lax.axis_size("tp") != 2:
        return lax.all_gather(projector, "tp", axis=0, tiled=True)
    t, c = lax.axis_index("tp"), lax.axis_index("sub")
    mine = halves(projector, 0, c)[0]
    got = swap(mine, "tp", 1)
    other = in_order(got, swap(got, "sub", 1), c, 0)
    return in_order(projector, other, t, 0)


def shards_any(hidden_acts, cotangent, w_down, projector, first_moment, second_moment):
    nz, nx = lax.axis_size("fsdp"), lax.axis_size("tp")
    z, t = lax.axis_index("fsdp"), lax.axis_index("tp")
    rows, width = hidden_acts.shape[0], w_down.shape[0]
    bits = [1 << b for b in range(nz.bit_length() - 1)]
    two = nx == 2

    cot = {0: cotangent}
    for bit in reversed(bits):
        for k in list(cot):
            cot[k ^ bit] = swap(cot[k], "fsdp", bit)
    hid = {}
    for k in range(nz):
        part = lax.dynamic_slice_in_dim(hidden_acts, (z ^ k) * width, width, 1)
        hid[k] = swap(part, "fsdp", k) if k else part

    basis = full_basis_of(projector)
    if two:
        w_mine, w_other = halves(w_down, 1, t)
        b_mine, b_other = halves(basis, 0, t)
        pairs = {k: ((cot[k], w_mine, b_mine), (swap(cot[k], "tp", 1), w_other, b_other)) for k in cot}
    else:
        pairs = {
            k: ((lax.all_gather(cot[k], "tp", axis=1, tiled=True), w_down, basis),) for k in cot
        }

    grads, coords = {}, {}
    for k in cot:
        back = sum(mm_t(c, w) for c, w, _ in pairs[k]).astype(bf16)
        grads[k] = swap(back, "fsdp", k) if k else back
        coords[k] = sum(mm(c, b) for c, _, b in pairs[k]).astype(bf16)
    order = jnp.stack([grads[k] for k in range(nz)])
    acts_grad = jnp.concatenate(
        [lax.dynamic_index_in_dim(order, z ^ j, 0, keepdims=False) for j in range(nz)], axis=1
    )

    outs = {}
    for k in range(nz):
        if two:
            away = mm(hid[k], w_other).astype(bf16)
            outs[k] = mm(hid[k], w_mine) + swap(away, "tp", 1).astype(f32)
        else:
            outs[k] = lax.psum_scatter(
                mm(hid[k], w_down).astype(bf16), "tp", scatter_dimension=1, tiled=True
            ).astype(f32)
    for bit in bits:
        for k in [k for k in outs if k & bit]:
            got = swap(outs.pop(k).astype(bf16), "fsdp", bit)
            outs[k ^ bit] = outs[k ^ bit] + got.astype(f32)
    block_out = outs[0].astype(bf16)

    all_hid = jnp.concatenate([hid[k] for k in range(nz)], axis=0)
    all_coords = jnp.concatenate([coords[k] for k in range(nz)], axis=0)
    local = mm_tn(all_hid, all_coords)
    owned = local + swap(local, "sub", 1)
    token_count = f32(rows * nz * lax.axis_size("sub"))
    direction, new_first, new_second = adam_rows(owned / token_count, first_moment, second_moment)
    weight_step = mm_t(direction, basis)
    return (block_out, acts_grad, weight_step, new_first, new_second)


light = pl.CostEstimate(flops=1, bytes_accessed=1, transcendentals=0)
strip = 512


def in_vmem(kernel, name, at, ins, outs, mib=12):
    vmem = pl.BlockSpec(memory_space=pltpu.VMEM)
    return pl.pallas_call(
        kernel,
        in_specs=[pl.BlockSpec(memory_space=pltpu.SMEM)] + [vmem] * len(ins),
        out_specs=[vmem] * len(outs),
        out_shape=outs,
        compiler_params=pltpu.CompilerParams(vmem_limit_bytes=mib << 20),
        cost_estimate=light,
        name=name,
    )(at, *ins)


def forward(at, h, w):
    rows, width = h.shape[0], w.shape[1]
    half = width // 2

    def kernel(at, h, w, p, m):
        mine, far = at[0] * half, (1 - at[0]) * half
        for j in range(0, half, strip):
            p[:, j : j + strip] = mm(h[...], w[:, pl.ds(pl.multiple_of(far + j, strip), strip)]).astype(bf16)
        for j in range(0, half, strip):
            m[:, j : j + strip] = mm(h[...], w[:, pl.ds(pl.multiple_of(mine + j, strip), strip)])

    return in_vmem(
        kernel, "forward", at, (h, w),
        [jax.ShapeDtypeStruct((rows, half), bf16), jax.ShapeDtypeStruct((rows, half), f32)],
    )


def backward(at, c, x, w, projector, got, shared):
    rows, half = c.shape
    units = w.shape[0]
    part = half // 2
    tall = 352

    def kernel(at, c, x, w, basis, got, shared, g, coords):
        mine = pl.multiple_of(at[0] * half, half)
        far = pl.multiple_of((1 - at[0]) * half, half)
        first = pl.multiple_of(at[1] * part, part)
        second = pl.multiple_of((1 - at[1]) * part, part)
        for j in range(0, units, tall):
            k = min(j + tall, units)
            g[j:k, :] = (
                mm_t(w[j:k, pl.ds(mine, half)], c[...]) + mm_t(w[j:k, pl.ds(far, half)], x[...])
            ).astype(bf16)
        coords[...] = (
            mm(c[...], basis[...])
            + mm(x[:, pl.ds(first, part)], got[...])
            + mm(x[:, pl.ds(second, part)], shared[...])
        ).astype(bf16)

    return in_vmem(
        kernel, "backward", at, (c, x, w, projector, got, shared),
        [
            jax.ShapeDtypeStruct((units, rows), bf16),
            jax.ShapeDtypeStruct((rows, projector.shape[1]), bf16),
        ],
    )


def project(at, hs, coords):
    n, units, rank = len(hs), hs[0].shape[1], coords[0].shape[1]
    tall = units // 2

    def kernel(at, *refs):
        upper, lower = refs[2 * n :]
        total = sum(mm_tn(h[...], c[...]) for h, c in zip(refs[:n], refs[n : 2 * n]))
        upper[...], lower[...] = total[:tall], total[tall:]

    return in_vmem(
        kernel, "project", at, (*hs, *coords), [jax.ShapeDtypeStruct((tall, rank), f32)] * 2
    )


def adam_step(at, here, there, tokens, first_moment, second_moment, projector, got, shared):
    units, rank = first_moment.shape
    half = projector.shape[0]
    part, width = half // 2, 2 * half
    tall = units // 4

    def kernel(at, h_up, h_low, t_up, t_low, first, second, basis, got, shared, step, new_first, new_second):
        upper = pl.program_id(0) < 2
        gradient = jnp.where(upper, h_up[...] + t_up[...], h_low[...] + t_low[...]) / f32(tokens)
        direction, new_first[...], new_second[...] = adam_rows(gradient, first[...], second[...])
        t, c = at[0], at[1]
        mine = pl.multiple_of(t * half, half)
        one = pl.multiple_of((1 - t) * half + c * part, part)
        two = pl.multiple_of((1 - t) * half + (1 - c) * part, part)
        step[:, pl.ds(mine, half)] = mm_t(direction, basis[...])
        step[:, pl.ds(one, part)] = mm_t(direction, got[...])
        step[:, pl.ds(two, part)] = mm_t(direction, shared[...])

    def block(index):
        return pl.BlockSpec((tall, rank), index)

    def up(i):
        return (jnp.minimum(i, 1), 0)

    def low(i):
        return (jnp.maximum(i, 2) - 2, 0)

    def row(i):
        return (i, 0)

    def whole(v):
        return pl.BlockSpec(v.shape, lambda i: (0, 0))

    small = jax.ShapeDtypeStruct((units, rank), f32)
    return pl.pallas_call(
        kernel,
        grid=(4,),
        in_specs=[pl.BlockSpec(memory_space=pltpu.SMEM)]
        + [block(up), block(low), block(up), block(low), block(row), block(row)]
        + [whole(projector), whole(got), whole(shared)],
        out_specs=[pl.BlockSpec((tall, width), row), block(row), block(row)],
        out_shape=[jax.ShapeDtypeStruct((units, width), f32), small, small],
        compiler_params=pltpu.CompilerParams(vmem_limit_bytes=24 << 20),
        cost_estimate=light,
        name="adam_step",
    )(at, *here, *there, first_moment, second_moment, projector, got, shared)


class Order:
    def __init__(self):
        self.last = ()

    def go(self, x):
        return lax.optimization_barrier((x, *self.last))[0]

    def seen(self, *done):
        self.last = done


def shards_line(hidden_acts, cotangent, w_down, projector, first_moment, second_moment):
    z, t, c = lax.axis_index("fsdp"), lax.axis_index("tp"), lax.axis_index("sub")
    rows, width = hidden_acts.shape[0], w_down.shape[0]
    at = jnp.stack([t, c]).astype(jnp.int32)
    tokens = rows * lax.axis_size("fsdp") * lax.axis_size("sub")
    order = Order()
    go, seen = order.go, order.seen

    def own_units(k):
        return lax.dynamic_slice_in_dim(hidden_acts, (z ^ k) * width, width, 1)

    c0 = cotangent
    c2 = swap(c0, "fsdp", 2, "c2")
    x0 = swap(c0, "tp", 1, "x0")
    h0, h1, h2, h3 = (own_units(k) for k in range(4))
    seen(h0)
    c1 = swap(go(c0), "fsdp", 1, "c1")
    half = swap(halves(go(projector), 0, c)[0], "tp", 1, "half")
    p0, m0 = forward(at, h0, w_down)
    seen(p0, c2)
    h3 = swap(go(h3), "fsdp", 3, "h3")
    x2 = swap(go(c2), "tp", 1, "x2")
    c3 = swap(go(c2), "fsdp", 1, "c3")
    seen(p0, c2, half, x0)
    basis = swap(go(half), "sub", 1, "basis")
    seen(p0, c1, x0, basis)
    x1 = swap(go(c1), "tp", 1, "x1")
    g0, k0 = backward(at, go(c0), x0, w_down, projector, half, basis)
    seen(g0, x2)
    g2, k2 = backward(at, go(c2), x2, w_down, projector, half, basis)
    seen(g2, h3)
    h2 = swap(go(h2), "fsdp", 2, "h2")
    h1 = swap(go(h1), "fsdp", 1, "h1")
    p3, m3 = forward(at, go(h3), w_down)
    seen(p3, c3)
    x3 = swap(go(c3), "tp", 1, "x3")
    seen(p3, c3, x1)
    g1, k1 = backward(at, go(c1), x1, w_down, projector, half, basis)
    seen(g1, h2)
    y3 = swap(go(p3), "tp", 1, "y3")
    a2 = swap(go(g2), "fsdp", 2, "a2")
    p2, m2 = forward(at, go(h2), w_down)
    seen(p2, h1)
    a1 = swap(go(g1), "fsdp", 1, "a1")
    p1, m1 = forward(at, go(h1), w_down)
    seen(p1, x3)
    y2 = swap(go(p2), "tp", 1, "y2")
    g3, k3 = backward(at, go(c3), x3, w_down, projector, half, basis)
    a3 = swap(g3, "fsdp", 3, "a3")
    seen(g3, y3, a2, a1)
    o3 = (go(m3) + y3.astype(f32)).astype(bf16)
    r3 = swap(o3, "fsdp", 1, "r3")
    y1 = swap(go(p1), "tp", 1, "y1")
    seen(o3)
    local = project(at, (h0, h1, h2, h3), (go(k0), k1, k2, k3))
    other = [swap(v, "sub", 1, "rows") for v in local]
    seen(local[0], y1, y2)
    o1 = (go(m1) + y1.astype(f32)).astype(bf16)
    r1 = swap(o1, "fsdp", 1, "r1")
    seen(o1, r3)
    o2 = (go(m2) + y2.astype(f32) + r3.astype(f32)).astype(bf16)
    r2 = swap(o2, "fsdp", 2, "r2")
    y0 = swap(go(p0), "tp", 1, "y0")
    seen(o2, a3)
    by_owner = jnp.stack([go(g0), a1, a2, a3])
    acts_grad = jnp.concatenate(
        [lax.dynamic_index_in_dim(by_owner, z ^ j, 0, keepdims=False) for j in range(4)], axis=0
    ).T
    seen(acts_grad)
    weight_step, new_first, new_second = adam_step(
        at, local, (go(other[0]), other[1]), tokens, first_moment, second_moment, projector, half, basis
    )
    seen(weight_step)
    o0 = go(m0) + y0.astype(f32) + r1.astype(f32)
    seen(o0)
    block_out = (o0 + go(r2).astype(f32)).astype(bf16)
    return (block_out, acts_grad, weight_step, new_first, new_second)


def solution(mesh):
    in_specs = (
        P(("groups", "fsdp", "sub"), "tp"),
        P(("groups", "fsdp", "sub"), "tp"),
        P(("tp", "fsdp"), None),
        P("tp", None),
        P(("groups", "tp", "fsdp"), None),
        P(("groups", "tp", "fsdp"), None),
    )
    out_specs = (
        P(("groups", "fsdp", "sub"), "tp"),
        P(("groups", "fsdp", "sub"), "tp"),
        P(("groups", "tp", "fsdp"), None),
        P(("groups", "tp", "fsdp"), None),
        P(("groups", "tp", "fsdp"), None),
    )
    line = mesh.shape["fsdp"] == 4 and mesh.shape["tp"] == 2
    shards = shards_line if line else shards_any
    return jax.shard_map(shards, mesh=mesh, in_specs=in_specs, out_specs=out_specs, check_vma=False)
```
